256 devices in a mesh: gx: 8 (over z), gy: 8 (over x, core), gz: 4 (over y).
Axes of the slice: x: 4, y: 4, z: 8, core: 2. Of those that a mesh axis runs over, the one named last changes fastest.
Arguments:
- rhs_interior: float32 [64, 8192, 512], P('gx', 'gy', 'gz'), may hold values from -9 to 9
- rhs_sep: float32 [8, 8192, 512], P('gx', 'gy', 'gz'), may hold values from -9 to 9
- lower_inv: float32 [64, 8, 4, 128, 128], P('gx', 'gy', 'gz'), may hold values from -1 to 1
- lower_off: float32 [56, 8, 4, 128, 128], P('gx', 'gy', 'gz'), may hold values from -4 to 1
- upper_inv: float32 [64, 8, 4, 128, 128], P('gx', 'gy', 'gz'), may hold values from -1 to 2
- upper_off: float32 [56, 8, 4, 128, 128], P('gx', 'gy', 'gz'), may hold values from -1 to 1
- link_into: float32 [16, 8192, 512], P('gx', 'gy', 'gz'), may hold values from 0.5 to 1.5
- link_from: float32 [16, 8192, 512], P('gx', 'gy', 'gz'), may hold values from 0.5 to 1.5
- sep_diag: float32 [8, 8192, 512], P('gx', 'gy', 'gz'), may hold values from 6 to 9
- coupling: int32 [4, 56, 8192], P('gz', 'gx', 'gy'), may hold values 0 or 1
Outputs:
- interior_solution: float32 [64, 8192, 512], P('gx', 'gy', 'gz')
- sep_solution: float32 [8, 8192, 512], P('gx', 'gy', 'gz')
The draws below stay inside these ranges and needn't reach their ends.
All inputs are finite; a program needn't handle non-finite values. No bound on the sum of `coupling` on one device may be relied on, other than what follows from the above.
Results may differ from the reference program's by a relative error of at most 0.0001.
Values sent between devices are 32-bit elements; how exact they have to be, the bound alone decides.
No kernel may reach another device: no remote copies, remote signals or barrier semaphores. Data moves between devices by JAX's collectives and lax.ppermute only.
A program may use at most 128 MiB of HBM per device.

```python
import jax
import jax.numpy as jnp
from jax import lax

CX = 8
CY = 1024
LINE = 128
OFFS = 7
PX = 8
PY = 8
PZ = 4
NXI = 64
NXO = 56
NY = 8192
NZ = 512


def source_field(key, rows, group):
    noise = jnp.clip(jax.random.normal(key, (rows, NY, NZ), jnp.float32), -5.0, 5.0)
    fraction = (jnp.arange(rows) // group).astype(jnp.float32) / max(PX - 1, 1)
    scale = 0.6 + 1.2 * fraction
    return noise * scale[:, None, None]


def factor_field(key, rows, diag_low, diag_high, spread):
    key_diag, key_rest = jax.random.split(key)
    diagonal = jax.random.uniform(key_diag, (rows, PY, PZ, LINE), jnp.float32, diag_low, diag_high)
    scatter = jnp.clip(jax.random.normal(key_rest, (rows, PY, PZ, LINE, LINE), jnp.float32), -4.0, 4.0)
    scatter = scatter * (spread * LINE ** (-0.5))
    return scatter + diagonal[..., None] * jnp.eye(LINE, dtype=jnp.float32)


def draw_rhs_interior(key, part):
    return source_field(jax.random.fold_in(key, 3), NXI, CX)


def draw_rhs_sep(key, part):
    return source_field(jax.random.fold_in(key, 5), PX, 1)


def draw_lower_inv(key, part):
    return factor_field(jax.random.fold_in(key, 11), NXI, 0.2, 0.4, 0.09)


def draw_lower_off(key, part):
    return factor_field(jax.random.fold_in(key, 13), NXO, -2.4, -1.6, 0.6)


def draw_upper_inv(key, part):
    return factor_field(jax.random.fold_in(key, 17), NXI, 0.7, 1.3, 0.3)


def draw_upper_off(key, part):
    return factor_field(jax.random.fold_in(key, 19), NXO, -0.6, -0.3, 0.14)


def with_ends(entries, stream_key, low, high):
    shape = entries.shape
    spot = [jax.random.randint(jax.random.fold_in(stream_key, axis), (), 0, shape[axis]) for axis in range(len(shape))]
    entries = entries.at[tuple(spot)].set(low)
    longest = shape.index(max(shape))
    spot[longest] = (spot[longest] + 1) % shape[longest]
    return entries.at[tuple(spot)].set(high)


def steps_of(stream_key, extent, pieces, smallest, largest):
    def one(dim, parts):
        draws = jax.random.uniform(jax.random.fold_in(jax.random.fold_in(stream_key, 6), dim), (parts,), jnp.float32, smallest / len(pieces), largest / len(pieces))
        return jnp.repeat(jnp.exp(draws), extent[dim] // parts).reshape((-1,) + (1,) * (len(extent) - dim - 1))

    level = one(*pieces[0])
    for cut in pieces[1:]:
        level = level * one(*cut)
    return level


def setup_inputs(seed: int = 0) -> dict:
    streams_of = jax.random.split(jax.random.key(seed), 11)
    return {
        "rhs_interior": draw_rhs_interior(jax.random.fold_in(streams_of[10], 71), 0),
        "rhs_sep": draw_rhs_sep(jax.random.fold_in(streams_of[10], 71), 0),
        "lower_inv": draw_lower_inv(jax.random.fold_in(streams_of[10], 71), 0),
        "lower_off": draw_lower_off(jax.random.fold_in(streams_of[10], 71), 0),
        "upper_inv": draw_upper_inv(jax.random.fold_in(streams_of[10], 71), 0),
        "upper_off": draw_upper_off(jax.random.fold_in(streams_of[10], 71), 0),
        "link_into": jnp.clip(0.5 + 1.0 * jax.random.uniform(streams_of[6], (2 * PX, NY, NZ), jnp.float32) ** steps_of(streams_of[6], (2 * PX, NY, NZ), ((0, 8), (1, 8), (2, 4)), -0.2, 0.2), 0.5, 1.5),
        "link_from": jnp.clip(0.5 + 1.0 * jax.random.uniform(streams_of[7], (2 * PX, NY, NZ), jnp.float32) ** steps_of(streams_of[7], (2 * PX, NY, NZ), ((0, 8), (1, 8), (2, 4)), -0.2, 0.2), 0.5, 1.5),
        "sep_diag": jnp.clip(6.0 + 3.0 * jax.random.uniform(streams_of[8], (PX, NY, NZ), jnp.float32) ** steps_of(streams_of[8], (PX, NY, NZ), ((0, 8), (1, 8), (2, 4)), -0.2, 0.2), 6.0, 9.0),
        "coupling": with_ends((jax.random.randint(streams_of[9], (PZ, NXO, NY), 0, 4) < 3).astype(jnp.int32), jax.random.fold_in(streams_of[9], 1), 0, 1),
    }


EPSILON = 1e-06
CONVECTION = 0.5

def multiply(left, right):
    return jnp.dot(left, right, precision=lax.Precision.HIGHEST, preferred_element_type=jnp.float32)

def sweep(sources, lower_inverse, lower_coupled, upper_inverse, upper_coupled, gating):
    planes = lower_inverse.shape[0]
    lowered = []
    running = None
    for position in range(planes):
        current = sources[position]
        if position > 0:
            current = current - gating[position - 1][:, None] * multiply(running, lower_coupled[position - 1])
        running = multiply(current, lower_inverse[position])
        lowered.append(running)
    solved = [None] * planes
    running = multiply(lowered[-1], upper_inverse[-1])
    solved[-1] = running
    for position in range(planes - 2, -1, -1):
        current = lowered[position] - gating[position][:, None] * multiply(running, upper_coupled[position])
        running = multiply(current, upper_inverse[position])
        solved[position] = running
    return solved

def interior_blocks(grid_field):
    return grid_field.reshape(PX, CX, PY, CY, PZ, LINE).transpose(0, 2, 4, 1, 3, 5).reshape(PX * PY * PZ, CX, CY, LINE)

def interior_field(blocks):
    return blocks.reshape(PX, PY, PZ, CX, CY, LINE).transpose(0, 3, 1, 4, 2, 5).reshape(NXI, NY, NZ)

def sep_blocks(grid_field):
    return grid_field.reshape(PX, PY, CY, PZ, LINE).transpose(0, 1, 3, 2, 4).reshape(PX * PY * PZ, CY, LINE)

def sep_field(blocks):
    return blocks.reshape(PX, PY, PZ, CY, LINE).transpose(0, 1, 3, 2, 4).reshape(PX, NY, NZ)

def factor_blocks(matrix, planes):
    return matrix.reshape(PX, planes, PY, PZ, LINE, LINE).transpose(0, 2, 3, 1, 4, 5).reshape(PX * PY * PZ, planes, LINE, LINE)

def gate_blocks(coupling):
    return coupling.reshape(PZ, PX, OFFS, PY, CY).transpose(1, 3, 0, 2, 4).reshape(PX * PY * PZ, OFFS, CY).astype(jnp.float32)

def shift_next(vector):
    return jnp.concatenate([vector[1:], jnp.zeros_like(vector[:1])], axis=0)

def shift_prev(vector):
    return jnp.concatenate([jnp.zeros_like(vector[:1]), vector[:-1]], axis=0)

def stencil(vector, sep_diag):
    padded = jnp.pad(vector, ((0, 0), (1, 1), (1, 1)))
    result = sep_diag * vector - (padded[:, :-2, 1:-1] + padded[:, 2:, 1:-1])
    return result - (1.0 + CONVECTION) * padded[:, 1:-1, :-2] - (1.0 - CONVECTION) * padded[:, 1:-1, 2:]

def least_squares(initial_norm, first_coeffs, first_norm, second_coeffs, second_norm):
    radius = jnp.sqrt(first_coeffs[0] * first_coeffs[0] + first_norm * first_norm)
    cosine = first_coeffs[0] / radius
    sine_value = first_norm / radius
    upper_entry = cosine * second_coeffs[0] + sine_value * second_coeffs[1]
    lower_entry = cosine * second_coeffs[1] - sine_value * second_coeffs[0]
    second_radius = jnp.sqrt(lower_entry * lower_entry + second_norm * second_norm)
    weight_two = -initial_norm * sine_value * lower_entry / (second_radius * second_radius)
    weight_one = (initial_norm * cosine - upper_entry * weight_two) / radius
    return (weight_one, weight_two)

def reference(rhs_interior, rhs_sep, lower_inv, lower_off, upper_inv, upper_off, link_into, link_from, sep_diag, coupling):
    factors = (factor_blocks(lower_inv, CX), factor_blocks(lower_off, OFFS), factor_blocks(upper_inv, CX), factor_blocks(upper_off, OFFS), gate_blocks(coupling))
    into_first = link_into[0::2]
    into_last = link_into[1::2]
    from_first = link_from[0::2]
    from_last = link_from[1::2]

    def ends_of(grouped):
        first_source, last_source, lower_a, lower_b, upper_a, upper_b, gate_rows = grouped
        empty_plane = jnp.zeros_like(first_source)
        sources = [first_source] + [empty_plane] * (CX - 2) + [last_source]
        solved = sweep(sources, lower_a, lower_b, upper_a, upper_b, gate_rows)
        return jnp.stack([solved[0], solved[-1]])

    def full_of(grouped):
        sources, lower_a, lower_b, upper_a, upper_b, gate_rows = grouped
        return jnp.stack(sweep(sources, lower_a, lower_b, upper_a, upper_b, gate_rows))

    def boundary_terms(first_plane, last_plane):
        return from_first * sep_field(first_plane) + shift_prev(from_last * sep_field(last_plane))

    def schur(vector):
        ends = lax.map(ends_of, (sep_blocks(into_first * vector), sep_blocks(into_last * shift_next(vector))) + factors)
        return stencil(vector, sep_diag) - boundary_terms(ends[:, 0], ends[:, 1])
    solved_all = lax.map(full_of, (interior_blocks(rhs_interior),) + factors)
    source = rhs_sep + boundary_terms(solved_all[:, 0], solved_all[:, -1])
    initial_norm = jnp.sqrt(jnp.sum(source * source) + EPSILON)
    basis_one = source / initial_norm
    image_one = schur(basis_one)
    first_coeffs = jnp.stack([jnp.sum(basis_one * image_one)])
    remainder = image_one - first_coeffs[0] * basis_one
    first_norm = jnp.sqrt(jnp.sum(remainder * remainder) + EPSILON)
    basis_two = remainder / first_norm
    image_two = schur(basis_two)
    second_coeffs = jnp.stack([jnp.sum(basis_one * image_two), jnp.sum(basis_two * image_two)])
    leftover = image_two - second_coeffs[0] * basis_one - second_coeffs[1] * basis_two
    second_norm = jnp.sqrt(jnp.sum(leftover * leftover) + EPSILON)
    weight_one, weight_two = least_squares(initial_norm, first_coeffs, first_norm, second_coeffs, second_norm)
    sep_solution = weight_one * basis_one + weight_two * basis_two
    blocks = interior_blocks(rhs_interior)
    blocks = blocks.at[:, 0].add(sep_blocks(into_first * sep_solution))
    blocks = blocks.at[:, -1].add(sep_blocks(into_last * shift_next(sep_solution)))
    interior_solution = interior_field(lax.map(full_of, (blocks,) + factors))
    return (interior_solution, sep_solution)
```

```python
import functools

import jax
import jax.numpy as jnp
from jax import lax
from jax.experimental import pallas as pl
from jax.experimental.pallas import tpu as pltpu
from jax.sharding import PartitionSpec as P

EPSILON = 1e-06
CONVECTION = 0.5
SHIFT = 7.5
SCALE_ONE = 2.0**-15
SCALE_TWO = 2.0**-30
AXES = ("gx", "gy", "gz")
LIMIT = 40 * 1024 * 1024

F32 = jnp.float32
BF16 = jnp.bfloat16


def halves(value):
    high = value.astype(BF16)
    low = (value - high.astype(F32)).astype(BF16)
    return high, low


def product(left, right):
    width = right[0].shape[1]
    wide = jnp.dot(left[0], jnp.concatenate(right, axis=1), preferred_element_type=F32)
    rest = jnp.dot(left[1], right[0], preferred_element_type=F32)
    return wide[:, :width] + (wide[:, width:] + rest)


def side(first, second):
    return tuple(jnp.concatenate([a, b], axis=1) for a, b in zip(first, second))


def over(first, second):
    return tuple(jnp.concatenate([a, b], axis=0) for a, b in zip(first, second))


def small(left, right):
    return product(halves(left), halves(right))


def masked(value, gate):
    return tuple(part * gate for part in value)


def column(gates, index, like):
    return jnp.broadcast_to(gates[:, index : index + 1], like).astype(BF16)


def forward_kernel(
    rhs_hbm, linv_hbm, loff_hbm, uinv_hbm, uoff_hbm, coupling_hbm, sep_hbm, from_hbm,
    m_ref, p_ref, t_ref, gates_ref, mats_ref,
    rhs, linv, loff, uinv, uoff, coupling, sep, link, sems,
):
    planes = rhs.shape[0]
    copies = {}

    def fetch(name, source, target):
        copies[name] = pltpu.make_async_copy(source, target, sems.at[len(copies)])
        copies[name].start()

    fetch("coupling", coupling_hbm.at[0], coupling)
    fetch("linv", linv_hbm.at[:, 0, 0], linv)
    fetch(0, rhs_hbm.at[0], rhs.at[0])
    fetch("loff", loff_hbm.at[:, 0, 0], loff)
    fetch("uinv", uinv_hbm.at[:, 0, 0], uinv)
    fetch("uoff", uoff_hbm.at[:, 0, 0], uoff)
    for plane in range(1, planes):
        fetch(plane, rhs_hbm.at[plane], rhs.at[plane])
    fetch("sep", sep_hbm.at[0], sep)
    fetch("link", from_hbm, link)

    copies["coupling"].wait()
    gate_rows = coupling[...].astype(F32)
    rows = [gate_rows[p : p + 1] for p in range(planes - 1)]
    prefix = [jnp.ones_like(rows[0])]
    for row in rows:
        prefix.append(prefix[-1] * row)
    open_any = [jnp.max(row, axis=1, keepdims=True) for row in prefix]
    gates = jnp.transpose(jnp.concatenate(rows + [jnp.zeros_like(rows[0])] + prefix, axis=0))
    gates_ref[...] = gates
    like = rhs.shape[1:]

    for name in ("linv", "loff", "uinv", "uoff"):
        copies[name].wait()
    lower = [halves(linv[p]) for p in range(planes)]
    upper = [halves(uinv[p]) for p in range(planes)]
    links_l, links_u = [None], []
    for p in range(1, planes):
        merged = product(halves(loff[p - 1]), lower[p])
        mats_ref[p - 1] = merged
        links_l.append(halves(merged))
    for p in range(planes - 1):
        merged = product(halves(uoff[p]), upper[p])
        mats_ref[planes - 1 + p] = merged
        links_u.append(halves(merged))
    back = [upper[0]]
    mats_ref[2 * planes - 2] = uinv[0]
    tail = None
    for p in range(1, planes):
        step = (-open_any[p]) * mats_ref[planes - 1 + p - 1]
        tail = step if tail is None else small(step, tail)
        full = product(upper[p], halves(tail))
        mats_ref[2 * planes - 2 + p] = full
        back.append(halves(full))

    total = None
    pending = None
    previous = None
    for p in range(planes):
        copies[p].wait()
        source = halves(rhs[p])
        if p == 0:
            running = product(source, lower[0])
        else:
            gated = masked(previous, -column(gates, p - 1, like))
            running = product(side(source, gated), over(lower[p], links_l[p]))
        t_ref[p] = running
        previous = halves(running)
        part = previous if p == 0 else masked(previous, column(gates, planes + p, like))
        if p % 2 == 0:
            pending = part
        else:
            term = product(side(pending, part), over(back[p - 1], back[p]))
            total = term if total is None else total + term
    copies["link"].wait()
    m_ref[...] = link[1] * product(previous, upper[planes - 1])
    copies["sep"].wait()
    p_ref[...] = sep[...] + link[0] * total


def backward_kernel(t_ref, gates_ref, mats_ref, linv_ref, uinv_ref, x_ref, apply_ref, sweep_ref):
    planes = t_ref.shape[0]
    gates = gates_ref[...]
    like = t_ref.shape[1:]
    upper = [halves(uinv_ref[p, 0, 0]) for p in range(planes)]
    links_u = [halves(mats_ref[planes - 1 + p]) for p in range(planes - 1)]
    size = like[1]

    def keep(ref, index, value):
        for part in range(2):
            ref[part, index * size : (index + 1) * size, :] = value[part]

    open_any = [jnp.max(gates[:, planes + p : planes + p + 1], axis=0, keepdims=True) for p in range(planes)]
    first = halves(linv_ref[0, 0, 0])
    last = halves(linv_ref[planes - 1, 0, 0])
    running = linv_ref[0, 0, 0]
    for p in range(planes):
        if p > 0:
            running = product(halves(running), halves((-open_any[p]) * mats_ref[p - 1]))
        now = halves(running) if p > 0 else first
        full = halves(mats_ref[2 * planes - 2 + p])
        keep(apply_ref, p, halves(product(now, full)))
        if p < planes - 1:
            keep(sweep_ref, 2 * p, halves(product(now, upper[p])))
            keep(sweep_ref, 2 * p + 1, links_u[p])
        else:
            keep(apply_ref, planes, halves(product(last, full)))
            keep(apply_ref, planes + 1, halves(product(last, upper[p])))
            keep(apply_ref, planes + 2, halves(product(now, upper[p])))

    solved = product(halves(t_ref[planes - 1]), upper[planes - 1])
    x_ref[planes - 1] = solved
    for p in range(planes - 2, -1, -1):
        gated = masked(halves(solved), -column(gates, p, like))
        solved = product(side(halves(t_ref[p]), gated), over(upper[p], links_u[p]))
        x_ref[p] = solved


def block(ref, first, count, size=128):
    return ref[0, first * size : (first + count) * size, :], ref[1, first * size : (first + count) * size, :]


def slab(vector, following, into_ref, gates, apply_ref):
    planes = 8
    like = vector.shape
    near = halves(into_ref[0] * vector)
    far = halves(into_ref[1] * following)
    cuts = [None] + [column(gates, planes + p, like) for p in range(1, planes)]
    gated = [near] + [masked(near, cuts[p]) for p in range(1, planes)]
    far_end = product(side(far, gated[-1]), block(apply_ref, planes + 1, 2))
    near_end = product(masked(far, cuts[-1]), block(apply_ref, planes, 1))
    for p in range(0, planes, 2):
        near_end = near_end + product(side(gated[p], gated[p + 1]), block(apply_ref, p, 2))
    return near_end, far_end


def inner_stencil(vector, diagonal):
    zero_row = jnp.zeros_like(vector[:1])
    zero_column = jnp.zeros_like(vector[:, :1])
    up = jnp.concatenate([zero_row, vector[:-1]], axis=0)
    down = jnp.concatenate([vector[1:], zero_row], axis=0)
    left = jnp.concatenate([zero_column, vector[:, :-1]], axis=1)
    right = jnp.concatenate([vector[:, 1:], zero_column], axis=1)
    return (
        (diagonal - SHIFT) * vector
        - (up + down)
        - (1.0 + CONVECTION) * left
        - (1.0 - CONVECTION) * right
    )


def put_rims(fields, rims):
    row_first, row_last, column_first, column_last = rims
    for index, field in enumerate(fields):
        row_first[index : index + 1, :] = field[:1]
        row_last[index : index + 1, :] = field[-1:]
        turned = jnp.transpose(field)
        column_first[index : index + 1, :] = turned[:1]
        column_last[index : index + 1, :] = turned[-1:]


def rim_columns(column_low, column_high):
    stacked = jnp.concatenate([column_low[...], column_high[...]] * 2, axis=0)
    return jnp.transpose(stacked)


def rim_terms(index, rows, turned, row_low, row_high, width):
    start, stop, total = rows
    count = stop - start
    lane = lax.broadcasted_iota(jnp.int32, (count, width), 1)
    line = lax.broadcasted_iota(jnp.int32, (count, width), 0)
    low = (1.0 + CONVECTION) * turned[start:stop, index : index + 1]
    high = (1.0 - CONVECTION) * turned[start:stop, index + 2 : index + 3]
    value = jnp.where(lane == 0, low, jnp.where(lane == width - 1, high, 0.0))
    if start == 0:
        value = value + jnp.where(line == 0, row_low[index : index + 1, :], 0.0)
    if stop == total:
        value = value + jnp.where(line == count - 1, row_high[index : index + 1, :], 0.0)
    return value


def first_kernel(
    flags, p_ref, m_ref, m_prev, p_next, into_ref, from_ref, diag_ref, gates_ref, apply_ref,
    k_ref, kn_ref, mm_ref, loc_ref, row_first, row_last, column_first, column_last,
):
    vector = p_ref[...] + m_prev[...]
    following = (p_next[...] + m_ref[...]) * flags[1]
    k_ref[...] = vector
    kn_ref[...] = following
    put_rims((vector, following), (row_first, row_last, column_first, column_last))
    near, far = slab(vector, following, into_ref, gates_ref[...], apply_ref)
    mm_ref[...] = from_ref[1] * far
    loc_ref[...] = inner_stencil(vector, diag_ref[0]) - from_ref[0] * near


def second_kernel(
    flags, loc_ref, mm_ref, mm_prev, loc_next, row_low, row_high, column_low, column_high,
    into_ref, from_ref, diag_ref, gates_ref, apply_ref,
    k_ref, kn_ref, mma_ref, mmb_ref, loca_ref, locb_ref, row_first, row_last, column_first, column_last,
):
    count, width = loc_ref.shape
    half = count // 2
    turned = rim_columns(column_low, column_high)
    rows = (0, count, count)
    vector = loc_ref[...] - mm_prev[...] - rim_terms(0, rows, turned, row_low, row_high, width)
    following = loc_next[...] - mm_ref[...] - rim_terms(1, rows, turned, row_low, row_high, width)
    following = following * flags[1]
    k_ref[...] = vector
    kn_ref[...] = following
    put_rims((vector, following), (row_first, row_last, column_first, column_last))
    near, far = slab(vector, following, into_ref, gates_ref[...], apply_ref)
    sent = from_ref[1] * far
    mma_ref[...] = sent[:half]
    mmb_ref[...] = sent[half:]
    local = inner_stencil(vector, diag_ref[0]) - from_ref[0] * near
    loca_ref[...] = local[:half]
    locb_ref[...] = local[half:]


def sums_kernel(
    flags, k0, k0n, k1, k1n, mma, mmb_prev, loca, locb, loca_next, row_low, row_high, column_low, column_high,
    out_ref,
):
    count, width = k0.shape
    half = count // 2
    turned = rim_columns(column_low, column_high)
    top, bottom = (0, half, count), (half, count, count)
    own_low = loca[...] - rim_terms(0, top, turned, row_low, row_high, width)
    own_high = locb[...] - mmb_prev[...] - rim_terms(0, bottom, turned, row_low, row_high, width)
    next_low = loca_next[...] - mma[...] - rim_terms(1, top, turned, row_low, row_high, width)
    groups = (
        (k0[half:], k1[half:] * SCALE_ONE, own_high * SCALE_TWO, None),
        (k0n[:half], k1n[:half] * SCALE_ONE, next_low * SCALE_TWO, flags[1]),
        (k0[:half], k1[:half] * SCALE_ONE, own_low * SCALE_TWO, flags[0]),
    )
    totals = [0.0] * 6
    for zero, one, two, weight in groups:
        pairs = ((zero, zero), (zero, one), (one, one), (zero, two), (one, two), (two, two))
        for index, (left, right) in enumerate(pairs):
            value = jnp.sum((left * right).reshape(half // 8, 8, width), axis=0)
            totals[index] = totals[index] + (value if weight is None else value * weight)
    lane = lax.broadcasted_iota(jnp.int32, (1, width), 1)
    line = jnp.zeros((1, width), F32)
    for index in range(6):
        line = jnp.where(lane == index, jnp.sum(totals[index]), line)
    out_ref[...] = line


def weights(sums):
    g00, g01, g11, g02, g12, g22 = sums
    one, two = 1.0 / SCALE_ONE, 1.0 / SCALE_TWO
    ratio = SCALE_ONE / SCALE_TWO
    square = g00 + EPSILON
    beta = jnp.sqrt(square)
    g00, g01s, g11s = g00 / square, g01 / square, g11 / square
    g02s, g12s, g22s = g02 / square, g12 / square, g22 / square
    lag = EPSILON / square
    delta = g01s * one - SHIFT * lag
    h11 = delta + SHIFT
    small_delta = delta * SCALE_ONE
    qq = (g11s - 2.0 * small_delta * g01s + small_delta * small_delta * g00) * one * one
    qq = jnp.maximum(qq, 0.0)
    h21 = jnp.sqrt(qq + EPSILON)
    inverse = 1.0 / h21
    gap = delta / ratio
    ku = (g02s - gap * g01s) * (two * inverse)
    kq = h11 * lag * inverse
    h12 = ku + SHIFT * kq
    qu = (g12s - gap * g11s - small_delta * g02s + small_delta * gap * g01s) * one * inverse * (two * inverse)
    vv = qq * inverse * inverse
    h22 = qu + SHIFT * vv
    turn = h22 - SHIFT
    uu = (g22s - 2.0 * gap * g12s + gap * gap * g11s) * (two * inverse) * (two * inverse)
    rr = uu + turn * turn * vv + h12 * h12 * g00 - 2.0 * turn * qu - 2.0 * h12 * ku + 2.0 * turn * h12 * kq
    h32 = jnp.sqrt(jnp.maximum(rr, 0.0) + EPSILON)
    radius = jnp.sqrt(h11 * h11 + h21 * h21)
    cosine = h11 / radius
    sine = h21 / radius
    upper_entry = cosine * h12 + sine * h22
    lower_entry = cosine * h22 - sine * h12
    second = jnp.sqrt(lower_entry * lower_entry + h32 * h32)
    weight_two = -beta * sine * lower_entry / (second * second)
    weight_one = (beta * cosine - upper_entry * weight_two) / radius
    scaled_two = weight_two * inverse / beta
    return weight_one / beta - scaled_two * delta, scaled_two


def final_kernel(
    gathered, k0, k0n, k1, k1n, into_ref, gates_ref, apply_ref, sweep_ref, x_ref,
    out_hbm, sep_hbm, out, sep, sems,
):
    planes = x_ref.shape[0]
    line = jnp.sum(gathered[...], axis=0, keepdims=True)
    lane = lax.broadcasted_iota(jnp.int32, line.shape, 1)
    sums = [jnp.sum(jnp.where(lane == index, line, 0.0), axis=1, keepdims=True) for index in range(6)]
    one, two = weights(sums)
    vector = one * k0[...] + two * k1[...]
    following = one * k0n[...] + two * k1n[...]
    sep[...] = vector
    copies = [pltpu.make_async_copy(sep, sep_hbm.at[0], sems.at[planes])]
    copies[0].start()
    gates = gates_ref[...]
    like = vector.shape
    near = halves(into_ref[0] * vector)
    far = halves(into_ref[1] * following)
    running = None
    for p in range(planes - 1, -1, -1):
        gated = near if p == 0 else masked(near, column(gates, planes + p, like))
        if running is None:
            running = product(side(far, gated), block(apply_ref, planes + 1, 2))
        else:
            other = masked(halves(running), -column(gates, p, like))
            running = product(side(gated, other), block(sweep_ref, 2 * p, 2))
        out[p] = x_ref[p] + running
        copies.append(pltpu.make_async_copy(out.at[p], out_hbm.at[p], sems.at[p]))
        copies[-1].start()
    for copy in copies:
        copy.wait()


def inside(count):
    return [pl.BlockSpec(memory_space=pltpu.VMEM)] * count


def outside(count):
    return [pl.BlockSpec(memory_space=pl.ANY)] * count


SCALARS = [pl.BlockSpec(memory_space=pltpu.SMEM)]


def shape(*sizes, dtype=F32):
    return jax.ShapeDtypeStruct(sizes, dtype)


def call(kernel, name, in_specs, out_shape, out_specs, scratch=(), flops=0, moved=0):
    return pl.pallas_call(
        kernel,
        name=name,
        in_specs=in_specs,
        out_shape=out_shape,
        out_specs=out_specs,
        scratch_shapes=list(scratch),
        compiler_params=pltpu.CompilerParams(vmem_limit_bytes=LIMIT),
        cost_estimate=pl.CostEstimate(flops=flops, bytes_accessed=moved, transcendentals=0),
    )


def body(
    rhs_interior, rhs_sep, lower_inv, lower_off, upper_inv, upper_off, link_into, link_from, sep_diag, coupling
):
    planes, count, width = rhs_interior.shape
    half = count // 2
    slabs, blocks, lines = (lax.axis_size(axis) for axis in AXES)
    place = lax.axis_index("gx")
    flags = jnp.stack([place == 0, place < slabs - 1]).astype(F32)
    plane = shape(count, width)
    dense = 2 * 2 * count * width * width

    def along(value, axis, by):
        size = lax.axis_size(axis)
        pairs = [(i, i + by) for i in range(size) if 0 <= i + by < size]
        return lax.ppermute(value, axis, pairs)

    def rims(row_first, row_last, column_first, column_last):
        return (
            along(row_last, "gy", 1),
            along(row_first, "gy", -1),
            along(column_last, "gz", 1),
            along(column_first, "gz", -1),
        )

    rim_shapes = [shape(2, width), shape(2, width), shape(2, count), shape(2, count)]

    m, p, t, gates, mats = call(
        forward_kernel,
        "forward",
        outside(8),
        [plane, plane, shape(planes, count, width), shape(count, 2 * planes), shape(3 * planes - 2, width, width)],
        inside(5),
        [
            pltpu.VMEM((planes, count, width), F32),
            pltpu.VMEM((planes, width, width), F32),
            pltpu.VMEM((planes - 1, width, width), F32),
            pltpu.VMEM((planes, width, width), F32),
            pltpu.VMEM((planes - 1, width, width), F32),
            pltpu.VMEM((planes - 1, count), jnp.int32),
            pltpu.VMEM((count, width), F32),
            pltpu.VMEM((2, count, width), F32),
            pltpu.SemaphoreType.DMA((planes + 7,)),
        ],
        flops=dense * 24,
        moved=12 << 20,
    )(rhs_interior, lower_inv, lower_off, upper_inv, upper_off, coupling, rhs_sep, link_from)
    m_prev = along(m, "gx", 1)
    p_next = along(p, "gx", -1)
    x, applied, swept = call(
        backward_kernel,
        "backward",
        inside(5),
        [
            shape(planes, count, width),
            shape(2, (planes + 3) * width, width, dtype=BF16),
            shape(2, (2 * planes - 2) * width, width, dtype=BF16),
        ],
        inside(3),
        flops=dense * 20,
        moved=12 << 20,
    )(t, gates, mats, lower_inv, upper_inv)
    k0, k0n, mm, loc, *edges = call(
        first_kernel,
        "first",
        SCALARS + inside(9),
        [plane] * 4 + rim_shapes,
        inside(8),
        flops=dense * 11,
        moved=4 << 20,
    )(flags, p, m, m_prev, p_next, link_into, link_from, sep_diag, gates, applied)
    mm_prev = along(mm, "gx", 1)
    loc_next = along(loc, "gx", -1)
    arrived = rims(*edges)
    part = shape(half, width)
    k1, k1n, mma, mmb, loca, locb, *edges = call(
        second_kernel,
        "second",
        SCALARS + inside(13),
        [plane] * 2 + [part] * 4 + rim_shapes,
        inside(10),
        flops=dense * 11,
        moved=4 << 20,
    )(flags, loc, mm, mm_prev, loc_next, *arrived, link_into, link_from, sep_diag, gates, applied)
    mmb_prev = along(mmb, "gx", 1)
    loca_next = along(loca, "gx", -1)
    arrived = rims(*edges)
    line = call(
        sums_kernel,
        "sums",
        SCALARS + inside(13),
        shape(1, width),
        pl.BlockSpec(memory_space=pltpu.VMEM),
        flops=dense,
        moved=4 << 20,
    )(flags, k0, k0n, k1, k1n, mma, mmb_prev, loca, locb, loca_next, *arrived)
    copies = jnp.broadcast_to(line, (slabs * blocks * lines, width))
    gathered = lax.all_to_all(copies, AXES, 0, 0, tiled=True)
    interior, separator = call(
        final_kernel,
        "final",
        inside(10),
        [shape(planes, count, width), shape(1, count, width)],
        outside(2),
        [
            pltpu.VMEM((planes, count, width), F32),
            pltpu.VMEM((count, width), F32),
            pltpu.SemaphoreType.DMA((planes + 1,)),
        ],
        flops=dense * 16,
        moved=12 << 20,
    )(gathered, k0, k0n, k1, k1n, link_into, gates, applied, swept, x)
    return interior, separator


def solution(mesh):
    field = P(*AXES)
    factor = P(*AXES, None, None)
    return jax.shard_map(
        body,
        mesh=mesh,
        in_specs=(field, field, factor, factor, factor, factor, field, field, field, P("gz", "gx", "gy")),
        out_specs=(field, field),
        check_vma=False,
    )
```

```python
import functools

import jax
import jax.numpy as jnp
from jax import lax
from jax.experimental import pallas as pl
from jax.experimental.pallas import tpu as pltpu
from jax.sharding import PartitionSpec as P

EPSILON = 1e-06
CONVECTION = 0.5
SHIFT = 7.5
SCALE_ONE = 2.0**-15
SCALE_TWO = 2.0**-30
AXES = ("gx", "gy", "gz")
LIMIT = 20 * 1024 * 1024

F32 = jnp.float32
BF16 = jnp.bfloat16


BEFORE, AFTER, ABOVE, BELOW, LEFT, RIGHT = range(6)


def neighbours():
    spots = [(lax.axis_index(axis), lax.axis_size(axis)) for axis in AXES]
    return [test for place, size in spots for test in (place > 0, place < size - 1)]


def only(flags, index, value):
    return jnp.where(flags[index], value, 0.0)


def halves(value):
    high = value.astype(BF16)
    low = (value - high.astype(F32)).astype(BF16)
    return high, low


def product(left, right):
    width = right[0].shape[1]
    wide = jnp.dot(left[0], jnp.concatenate(right, axis=1), preferred_element_type=F32)
    rest = jnp.dot(left[1], right[0], preferred_element_type=F32)
    return wide[:, :width] + (wide[:, width:] + rest)


def side(first, second):
    return tuple(jnp.concatenate([a, b], axis=1) for a, b in zip(first, second))


def over(first, second):
    return tuple(jnp.concatenate([a, b], axis=0) for a, b in zip(first, second))


def small(left, right):
    return product(halves(left), halves(right))


def masked(value, gate):
    return tuple(part * gate for part in value)


def column(gates, index, like):
    return jnp.broadcast_to(gates[:, index : index + 1], like).astype(BF16)


def forward_kernel(
    rhs_hbm, linv_hbm, loff_hbm, uinv_hbm, uoff_hbm, coupling_hbm, sep_hbm, from_hbm,
    m_ref, p_ref, t_ref, gates_ref, mats_ref,
    rhs, linv, loff, uinv, uoff, coupling, sep, link, sems,
):
    planes = rhs.shape[0]
    copies = {}

    def fetch(name, source, target):
        copies[name] = pltpu.make_async_copy(source, target, sems.at[len(copies)])
        copies[name].start()

    fetch("coupling", coupling_hbm.at[0], coupling)
    fetch("linv", linv_hbm.at[:, 0, 0], linv)
    fetch(0, rhs_hbm.at[0], rhs.at[0])
    fetch("loff", loff_hbm.at[:, 0, 0], loff)
    fetch("uinv", uinv_hbm.at[:, 0, 0], uinv)
    fetch("uoff", uoff_hbm.at[:, 0, 0], uoff)
    for plane in range(1, planes):
        fetch(plane, rhs_hbm.at[plane], rhs.at[plane])
    fetch("sep", sep_hbm.at[0], sep)
    fetch("link", from_hbm, link)

    copies["coupling"].wait()
    gate_rows = coupling[...].astype(F32)
    rows = [gate_rows[p : p + 1] for p in range(planes - 1)]
    prefix = [jnp.ones_like(rows[0])]
    for row in rows:
        prefix.append(prefix[-1] * row)
    open_any = [jnp.max(row, axis=1, keepdims=True) for row in prefix]
    gates = jnp.transpose(jnp.concatenate(rows + [jnp.zeros_like(rows[0])] + prefix, axis=0))
    gates_ref[...] = gates
    like = rhs.shape[1:]

    for name in ("linv", "loff", "uinv", "uoff"):
        copies[name].wait()
    lower = [halves(linv[p]) for p in range(planes)]
    upper = [halves(uinv[p]) for p in range(planes)]
    links_l, links_u = [None], []
    for p in range(1, planes):
        merged = product(halves(loff[p - 1]), lower[p])
        mats_ref[p - 1] = merged
        links_l.append(halves(merged))
    for p in range(planes - 1):
        merged = product(halves(uoff[p]), upper[p])
        mats_ref[planes - 1 + p] = merged
        links_u.append(halves(merged))
    back = [upper[0]]
    mats_ref[2 * planes - 2] = uinv[0]
    tail = None
    for p in range(1, planes):
        step = (-open_any[p]) * mats_ref[planes - 1 + p - 1]
        tail = step if tail is None else small(step, tail)
        full = product(upper[p], halves(tail))
        mats_ref[2 * planes - 2 + p] = full
        back.append(halves(full))

    total = None
    pending = None
    previous = None
    for p in range(planes):
        copies[p].wait()
        source = halves(rhs[p])
        if p == 0:
            running = product(source, lower[0])
        else:
            gated = masked(previous, -column(gates, p - 1, like))
            running = product(side(source, gated), over(lower[p], links_l[p]))
        t_ref[p] = running
        previous = halves(running)
        part = previous if p == 0 else masked(previous, column(gates, planes + p, like))
        if p % 2 == 0:
            pending = part
        else:
            term = product(side(pending, part), over(back[p - 1], back[p]))
            total = term if total is None else total + term
    copies["link"].wait()
    m_ref[...] = link[1] * product(previous, upper[planes - 1])
    copies["sep"].wait()
    p_ref[...] = sep[...] + link[0] * total


def backward_kernel(t_ref, gates_ref, mats_ref, linv_ref, uinv_ref, x_ref, apply_ref, sweep_ref, mask_ref):
    planes = t_ref.shape[0]
    gates = gates_ref[...]
    like = t_ref.shape[1:]
    upper = [halves(uinv_ref[p, 0, 0]) for p in range(planes)]
    links_u = [halves(mats_ref[planes - 1 + p]) for p in range(planes - 1)]
    size = like[1]

    def keep(ref, index, value):
        for part in range(2):
            ref[part, index * size : (index + 1) * size, :] = value[part]

    open_any = [jnp.max(gates[:, planes + p : planes + p + 1], axis=0, keepdims=True) for p in range(planes)]
    first = halves(linv_ref[0, 0, 0])
    last = halves(linv_ref[planes - 1, 0, 0])
    running = linv_ref[0, 0, 0]
    for p in range(planes):
        if p > 0:
            running = product(halves(running), halves((-open_any[p]) * mats_ref[p - 1]))
        now = halves(running) if p > 0 else first
        full = halves(mats_ref[2 * planes - 2 + p])
        keep(apply_ref, p, halves(product(now, full)))
        if p < planes - 1:
            keep(sweep_ref, 2 * p, halves(product(now, upper[p])))
            keep(sweep_ref, 2 * p + 1, links_u[p])
        else:
            keep(apply_ref, planes, halves(product(last, full)))
            keep(apply_ref, planes + 1, halves(product(last, upper[p])))
            keep(apply_ref, planes + 2, halves(product(now, upper[p])))

    solved = product(halves(t_ref[planes - 1]), upper[planes - 1])
    x_ref[planes - 1] = solved
    for p in range(planes - 2, -1, -1):
        mask = -column(gates, p, like)
        mask_ref[p] = mask
        solved = product(side(halves(t_ref[p]), masked(halves(solved), mask)), over(upper[p], links_u[p]))
        x_ref[p] = solved
    for p in range(1, planes):
        mask_ref[planes - 2 + p] = column(gates, planes + p, like)


def block(ref, first, count, size=128):
    return ref[0, first * size : (first + count) * size, :], ref[1, first * size : (first + count) * size, :]


def slab(vector, following, into_ref, mask_ref, apply_ref):
    planes = 8
    near = halves(into_ref[0] * vector)
    far = halves(into_ref[1] * following)
    gated = [near] + [masked(near, mask_ref[planes - 2 + p]) for p in range(1, planes)]
    far_end = product(side(far, gated[-1]), block(apply_ref, planes + 1, 2))
    near_end = product(masked(far, mask_ref[2 * planes - 3]), block(apply_ref, planes, 1))
    for p in range(0, planes, 2):
        near_end = near_end + product(side(gated[p], gated[p + 1]), block(apply_ref, p, 2))
    return near_end, far_end


def inner_stencil(vector, diagonal):
    zero_row = jnp.zeros_like(vector[:1])
    zero_column = jnp.zeros_like(vector[:, :1])
    up = jnp.concatenate([zero_row, vector[:-1]], axis=0)
    down = jnp.concatenate([vector[1:], zero_row], axis=0)
    left = jnp.concatenate([zero_column, vector[:, :-1]], axis=1)
    right = jnp.concatenate([vector[:, 1:], zero_column], axis=1)
    return (
        (diagonal - SHIFT) * vector
        - (up + down)
        - (1.0 + CONVECTION) * left
        - (1.0 - CONVECTION) * right
    )


def put_rims(fields, rims):
    row_first, row_last, column_first, column_last = rims
    for index, field in enumerate(fields):
        row_first[index : index + 1, :] = field[:1]
        row_last[index : index + 1, :] = field[-1:]
        turned = jnp.transpose(field)
        column_first[index : index + 1, :] = turned[:1]
        column_last[index : index + 1, :] = turned[-1:]


def rim_columns(flags, column_low, column_high):
    low = (1.0 + CONVECTION) * only(flags, LEFT, column_low[...])
    high = (1.0 - CONVECTION) * only(flags, RIGHT, column_high[...])
    return jnp.transpose(jnp.concatenate([low, high] * 2, axis=0))


def rim_terms(flags, index, rows, turned, row_low, row_high, width):
    start, stop, total = rows
    count = stop - start
    lane = lax.broadcasted_iota(jnp.int32, (count, width), 1)
    line = lax.broadcasted_iota(jnp.int32, (count, width), 0)
    low = turned[start:stop, index : index + 1]
    high = turned[start:stop, index + 2 : index + 3]
    value = jnp.where(lane == 0, low, jnp.where(lane == width - 1, high, 0.0))
    if start == 0:
        value = value + jnp.where(line == 0, only(flags, ABOVE, row_low[index : index + 1, :]), 0.0)
    if stop == total:
        value = value + jnp.where(line == count - 1, only(flags, BELOW, row_high[index : index + 1, :]), 0.0)
    return value


def first_kernel(
    p_ref, m_ref, m_prev, p_next, into_ref, from_ref, diag_ref, mask_ref, apply_ref,
    k_ref, kn_ref, mm_ref, loc_ref, row_first, row_last, column_first, column_last,
):
    flags = neighbours()
    vector = p_ref[...] + only(flags, BEFORE, m_prev[...])
    following = only(flags, AFTER, p_next[...] + m_ref[...])
    k_ref[...] = vector
    kn_ref[...] = following
    put_rims((vector, following), (row_first, row_last, column_first, column_last))
    near, far = slab(vector, following, into_ref, mask_ref, apply_ref)
    mm_ref[...] = from_ref[1] * far
    loc_ref[...] = inner_stencil(vector, diag_ref[0]) - from_ref[0] * near


def second_kernel(
    loc_ref, mm_ref, mm_prev, loc_next, row_low, row_high, column_low, column_high,
    into_ref, from_ref, diag_ref, mask_ref, apply_ref,
    k_ref, kn_ref, mma_ref, mmb_ref, loca_ref, locb_ref, row_first, row_last, column_first, column_last,
):
    flags = neighbours()
    count, width = loc_ref.shape
    half = count // 2
    turned = rim_columns(flags, column_low, column_high)
    rows = (0, count, count)
    vector = loc_ref[...] - only(flags, BEFORE, mm_prev[...]) - rim_terms(flags, 0, rows, turned, row_low, row_high, width)
    following = loc_next[...] - mm_ref[...] - rim_terms(flags, 1, rows, turned, row_low, row_high, width)
    following = only(flags, AFTER, following)
    k_ref[...] = vector
    kn_ref[...] = following
    put_rims((vector, following), (row_first, row_last, column_first, column_last))
    near, far = slab(vector, following, into_ref, mask_ref, apply_ref)
    sent = from_ref[1] * far
    mma_ref[...] = sent[:half]
    mmb_ref[...] = sent[half:]
    local = inner_stencil(vector, diag_ref[0]) - from_ref[0] * near
    loca_ref[...] = local[:half]
    locb_ref[...] = local[half:]


def sums_kernel(
    k0, k0n, k1, k1n, mma, mmb_prev, loca, locb, loca_next, row_low, row_high, column_low, column_high, x0_ref, x1_ref,
    out_ref,
):
    flags = neighbours()
    count, width = k0.shape
    half = count // 2
    turned = rim_columns(flags, column_low, column_high)
    top, bottom = (0, half, count), (half, count, count)
    own_low = loca[...] - rim_terms(flags, 0, top, turned, row_low, row_high, width)
    own_high = locb[...] - only(flags, BEFORE, mmb_prev[...]) - rim_terms(flags, 0, bottom, turned, row_low, row_high, width)
    next_low = loca_next[...] - mma[...] - rim_terms(flags, 1, top, turned, row_low, row_high, width)
    groups = (
        (k0[half:], k1[half:] * SCALE_ONE, own_high * SCALE_TWO),
        (k0n[:half], k1n[:half] * SCALE_ONE, only(flags, AFTER, next_low) * SCALE_TWO),
        (k0[:half], k1[:half] * SCALE_ONE, own_low * SCALE_TWO),
    )
    totals = [0.0] * 6
    for ordinal, (zero, one, two) in enumerate(groups):
        pairs = ((zero, zero), (zero, one), (one, one), (zero, two), (one, two), (two, two))
        for index, (left, right) in enumerate(pairs):
            value = jnp.sum((left * right).reshape(half // 8, 8, width), axis=0)
            if ordinal == 2:
                value = jnp.where(flags[BEFORE], 0.0, value)
            totals[index] = totals[index] + value
    lane = lax.broadcasted_iota(jnp.int32, (1, width), 1)
    line = jnp.zeros((1, width), F32)
    for index in range(6):
        line = jnp.where(lane == index, jnp.sum(totals[index]), line)
    out_ref[...] = jnp.broadcast_to(line, out_ref.shape)


def weights(sums):
    g00, g01, g11, g02, g12, g22 = sums
    one, two = 1.0 / SCALE_ONE, 1.0 / SCALE_TWO
    ratio = SCALE_ONE / SCALE_TWO
    square = g00 + EPSILON
    beta = jnp.sqrt(square)
    g00, g01s, g11s = g00 / square, g01 / square, g11 / square
    g02s, g12s, g22s = g02 / square, g12 / square, g22 / square
    lag = EPSILON / square
    delta = g01s * one - SHIFT * lag
    h11 = delta + SHIFT
    small_delta = delta * SCALE_ONE
    qq = (g11s - 2.0 * small_delta * g01s + small_delta * small_delta * g00) * one * one
    qq = jnp.maximum(qq, 0.0)
    h21 = jnp.sqrt(qq + EPSILON)
    inverse = 1.0 / h21
    gap = delta / ratio
    ku = (g02s - gap * g01s) * (two * inverse)
    kq = h11 * lag * inverse
    h12 = ku + SHIFT * kq
    qu = (g12s - gap * g11s - small_delta * g02s + small_delta * gap * g01s) * one * inverse * (two * inverse)
    vv = qq * inverse * inverse
    h22 = qu + SHIFT * vv
    turn = h22 - SHIFT
    uu = (g22s - 2.0 * gap * g12s + gap * gap * g11s) * (two * inverse) * (two * inverse)
    rr = uu + turn * turn * vv + h12 * h12 * g00 - 2.0 * turn * qu - 2.0 * h12 * ku + 2.0 * turn * h12 * kq
    h32 = jnp.sqrt(jnp.maximum(rr, 0.0) + EPSILON)
    radius = jnp.sqrt(h11 * h11 + h21 * h21)
    cosine = h11 / radius
    sine = h21 / radius
    upper_entry = cosine * h12 + sine * h22
    lower_entry = cosine * h22 - sine * h12
    second = jnp.sqrt(lower_entry * lower_entry + h32 * h32)
    weight_two = -beta * sine * lower_entry / (second * second)
    weight_one = (beta * cosine - upper_entry * weight_two) / radius
    scaled_two = weight_two * inverse / beta
    return weight_one / beta - scaled_two * delta, scaled_two


def sweep_kernel(k, kn, into_ref, mask_ref, apply_ref, sweep_ref, x_ref):
    planes = x_ref.shape[0]
    near = halves(into_ref[0] * k[...])
    far = halves(into_ref[1] * kn[...])
    running = None
    for p in range(planes - 1, -1, -1):
        gated = near if p == 0 else masked(near, mask_ref[planes - 2 + p])
        if running is None:
            running = product(side(far, gated), block(apply_ref, planes + 1, 2))
        else:
            other = masked(halves(running), mask_ref[p])
            running = product(side(gated, other), block(sweep_ref, 2 * p, 2))
        x_ref[p] = running


def final_kernel(gathered, k0, k1, x_ref, x0_ref, x1_ref, out_hbm, sep_hbm, out, sep, sems):
    planes = x_ref.shape[0]
    line = jnp.sum(gathered[...], axis=0, keepdims=True)
    lane = lax.broadcasted_iota(jnp.int32, line.shape, 1)
    sums = [jnp.sum(jnp.where(lane == index, line, 0.0), axis=1, keepdims=True) for index in range(6)]
    one, two = weights(sums)
    copies = []
    for p in range(planes):
        out[p] = x_ref[p] + (one * x0_ref[p] + two * x1_ref[p])
        copies.append(pltpu.make_async_copy(out.at[p], out_hbm.at[p], sems.at[p]))
        copies[-1].start()
    sep[...] = one * k0[...] + two * k1[...]
    copies.append(pltpu.make_async_copy(sep, sep_hbm.at[0], sems.at[planes]))
    copies[-1].start()
    for copy in copies:
        copy.wait()


def inside(count):
    return [pl.BlockSpec(memory_space=pltpu.VMEM)] * count


def outside(count, space=pl.ANY):
    return [pl.BlockSpec(memory_space=space)] * count


def shape(*sizes, dtype=F32):
    return jax.ShapeDtypeStruct(sizes, dtype)


def call(kernel, name, in_specs, out_shape, out_specs, scratch=(), flops=0, moved=0):
    return pl.pallas_call(
        kernel,
        name=name,
        in_specs=in_specs,
        out_shape=out_shape,
        out_specs=out_specs,
        scratch_shapes=list(scratch),
        compiler_params=pltpu.CompilerParams(vmem_limit_bytes=LIMIT),
        cost_estimate=pl.CostEstimate(flops=flops, bytes_accessed=moved, transcendentals=0),
    )


def body(
    rhs_interior, rhs_sep, lower_inv, lower_off, upper_inv, upper_off, link_into, link_from, sep_diag, coupling
):
    planes, count, width = rhs_interior.shape
    half = count // 2
    slabs, blocks, lines = (lax.axis_size(axis) for axis in AXES)
    plane = shape(count, width)
    dense = 2 * 2 * count * width * width

    def along(value, axis, by):
        size = lax.axis_size(axis)
        return lax.ppermute(value, axis, [(i, (i + by) % size) for i in range(size)])

    def rims(row_first, row_last, column_first, column_last):
        return (
            along(row_last, "gy", 1),
            along(row_first, "gy", -1),
            along(column_last, "gz", 1),
            along(column_first, "gz", -1),
        )

    rim_shapes = [shape(2, width), shape(2, width), shape(2, count), shape(2, count)]

    m, p, t, gates, mats = call(
        forward_kernel,
        "forward",
        outside(8, pltpu.HBM),
        [plane, plane, shape(planes, count, width), shape(count, 2 * planes), shape(3 * planes - 2, width, width)],
        inside(5),
        [
            pltpu.VMEM((planes, count, width), F32),
            pltpu.VMEM((planes, width, width), F32),
            pltpu.VMEM((planes - 1, width, width), F32),
            pltpu.VMEM((planes, width, width), F32),
            pltpu.VMEM((planes - 1, width, width), F32),
            pltpu.VMEM((planes - 1, count), jnp.int32),
            pltpu.VMEM((count, width), F32),
            pltpu.VMEM((2, count, width), F32),
            pltpu.SemaphoreType.DMA((planes + 7,)),
        ],
        flops=dense * 24,
        moved=12 << 20,
    )(*(
        pltpu.with_memory_space_constraint(array, pltpu.HBM)
        for array in (rhs_interior, lower_inv, lower_off, upper_inv, upper_off, coupling, rhs_sep, link_from)
    ))
    m_prev = along(m, "gx", 1)
    p_next = along(p, "gx", -1)
    x, applied, swept, masks = call(
        backward_kernel,
        "backward",
        inside(5),
        [
            shape(planes, count, width),
            shape(2, (planes + 3) * width, width, dtype=BF16),
            shape(2, (2 * planes - 2) * width, width, dtype=BF16),
            shape(2 * planes - 2, count, width, dtype=BF16),
        ],
        inside(4),
        flops=dense * 20,
        moved=12 << 20,
    )(t, gates, mats, lower_inv, upper_inv)
    k0, k0n, mm, loc, *edges = call(
        first_kernel,
        "first",
        inside(9),
        [plane] * 4 + rim_shapes,
        inside(8),
        flops=dense * 11,
        moved=4 << 20,
    )(p, m, m_prev, p_next, link_into, link_from, sep_diag, masks, applied)
    mm_prev = along(mm, "gx", 1)
    loc_next = along(loc, "gx", -1)
    arrived = rims(*edges)

    def swept_field(name, k, kn):
        return call(
            sweep_kernel,
            name,
            inside(6),
            shape(planes, count, width),
            pl.BlockSpec(memory_space=pltpu.VMEM),
            flops=dense * 16,
            moved=8 << 20,
        )(k, kn, link_into, masks, applied, swept)

    x0 = swept_field("sweep_first", k0, k0n)
    part = shape(half, width)
    k1, k1n, mma, mmb, loca, locb, *edges = call(
        second_kernel,
        "second",
        inside(13),
        [plane] * 2 + [part] * 4 + rim_shapes,
        inside(10),
        flops=dense * 11,
        moved=4 << 20,
    )(loc, mm, mm_prev, loc_next, *arrived, link_into, link_from, sep_diag, masks, applied)
    mmb_prev = along(mmb, "gx", 1)
    loca_next = along(loca, "gx", -1)
    arrived = rims(*edges)
    x1 = swept_field("sweep_second", k1, k1n)
    line = call(
        sums_kernel,
        "sums",
        inside(13) + outside(2),
        shape(slabs * blocks * lines, width),
        pl.BlockSpec(memory_space=pltpu.VMEM),
        flops=dense,
        moved=4 << 20,
    )(k0, k0n, k1, k1n, mma, mmb_prev, loca, locb, loca_next, *arrived, x0, x1)
    gathered = lax.all_to_all(line, AXES, 0, 0, tiled=True)
    interior, separator = call(
        final_kernel,
        "final",
        inside(6),
        [shape(planes, count, width), shape(1, count, width)],
        outside(2),
        [
            pltpu.VMEM((planes, count, width), F32),
            pltpu.VMEM((count, width), F32),
            pltpu.SemaphoreType.DMA((planes + 1,)),
        ],
        flops=dense,
        moved=16 << 20,
    )(gathered, k0, k1, x, x0, x1)
    return interior, separator


def solution(mesh):
    field = P(*AXES)
    factor = P(*AXES, None, None)
    return jax.shard_map(
        body,
        mesh=mesh,
        in_specs=(field, field, factor, factor, factor, factor, field, field, field, P("gz", "gx", "gy")),
        out_specs=(field, field),
        check_vma=False,
    )
```

```python
import functools

import jax
import jax.numpy as jnp
from jax import lax
from jax.experimental import pallas as pl
from jax.experimental.pallas import tpu as pltpu
from jax.sharding import PartitionSpec as P

EPSILON = 1e-06
CONVECTION = 0.5
SHIFT = 7.5
SCALE_ONE = 2.0**-15
SCALE_TWO = 2.0**-30
AXES = ("gx", "gy", "gz")
LIMIT = 20 * 1024 * 1024

F32 = jnp.float32
BF16 = jnp.bfloat16


BEFORE, AFTER, ABOVE, BELOW, LEFT, RIGHT = range(6)


def neighbours():
    spots = [(lax.axis_index(axis), lax.axis_size(axis)) for axis in AXES]
    return [test for place, size in spots for test in (place > 0, place < size - 1)]


def only(flags, index, value):
    return jnp.where(flags[index], value, 0.0)


def halves(value):
    high = value.astype(BF16)
    low = (value - high.astype(F32)).astype(BF16)
    return high, low


def product(left, right):
    width = right[0].shape[1]
    wide = jnp.dot(left[0], jnp.concatenate(right, axis=1), preferred_element_type=F32)
    rest = jnp.dot(left[1], right[0], preferred_element_type=F32)
    return wide[:, :width] + (wide[:, width:] + rest)


def side(first, second):
    return tuple(jnp.concatenate([a, b], axis=1) for a, b in zip(first, second))


def over(first, second):
    return tuple(jnp.concatenate([a, b], axis=0) for a, b in zip(first, second))


def small(left, right):
    return product(halves(left), halves(right))


def masked(value, gate):
    return tuple(part * gate for part in value)


def column(gates, index, like):
    return jnp.broadcast_to(gates[:, index : index + 1], like).astype(BF16)


def block(ref, first, count, size=128):
    return ref[0, first * size : (first + count) * size, :], ref[1, first * size : (first + count) * size, :]


def keep(ref, index, value):
    size = value[0].shape[0]
    for part in range(2):
        ref[part, index * size : (index + 1) * size, :] = value[part]


def fetcher(sems):
    copies = {}

    def fetch(name, source, target):
        copies[name] = pltpu.make_async_copy(source, target, sems.at[len(copies)])
        copies[name].start()

    return copies, fetch


def forward_rows(copies, rhs, t_ref, gates, lower_ref, back_ref, upper_ref, link, sep, m_ref, p_ref):
    planes = rhs.shape[0]
    like = rhs.shape[1:]
    total = None
    pending = None
    previous = None
    for p in range(planes):
        copies[p].wait()
        source = halves(rhs[p])
        if p == 0:
            running = product(source, block(lower_ref, 0, 1))
        else:
            gated = masked(previous, -column(gates, p - 1, like))
            running = product(side(source, gated), block(lower_ref, 2 * p - 1, 2))
        t_ref[p] = running
        previous = halves(running)
        part = previous if p == 0 else masked(previous, column(gates, planes + p, like))
        if p % 2 == 0:
            pending = part
        else:
            term = product(side(pending, part), block(back_ref, p - 1, 2))
            total = term if total is None else total + term
    copies["link"].wait()
    m_ref[...] = link[1] * product(previous, block(upper_ref, 2 * planes - 2, 1))
    copies["sep"].wait()
    p_ref[...] = sep[...] + link[0] * total


def forward_kernel(
    rhs_hbm, linv_hbm, loff_hbm, uinv_hbm, uoff_hbm, coupling_hbm, sep_hbm, from_hbm,
    m_ref, p_ref, t_ref, gates_ref, lower_ref, upper_ref, back_ref,
    rhs, linv, loff, uinv, uoff, coupling, sep, link, sems,
):
    planes, count, _ = rhs.shape
    copies, fetch = fetcher(sems)
    fetch("coupling", coupling_hbm, coupling)
    fetch("linv", linv_hbm.at[:, 0, 0], linv)
    fetch("loff", loff_hbm.at[:, 0, 0], loff)
    fetch("uinv", uinv_hbm.at[:, 0, 0], uinv)
    fetch("uoff", uoff_hbm.at[:, 0, 0], uoff)
    for plane in range(planes):
        fetch(plane, rhs_hbm.at[plane, :count], rhs.at[plane])
    fetch("link", from_hbm.at[:, :count], link)
    fetch("sep", sep_hbm.at[0, :count], sep)

    copies["coupling"].wait()
    tiles = coupling[...].astype(F32)
    rows = [
        jnp.concatenate([tiles[p, q : q + 1] for q in range(tiles.shape[1])], axis=1) for p in range(planes - 1)
    ]
    prefix = [jnp.ones_like(rows[0])]
    for row in rows:
        prefix.append(prefix[-1] * row)
    open_any = [jnp.max(row, axis=1, keepdims=True) for row in prefix]
    gates = jnp.transpose(jnp.concatenate(rows + [jnp.zeros_like(rows[0])] + prefix, axis=0))
    gates_ref[...] = gates

    for name in ("linv", "loff", "uinv", "uoff"):
        copies[name].wait()
    lower = [halves(linv[p]) for p in range(planes)]
    upper = [halves(uinv[p]) for p in range(planes)]
    keep(lower_ref, 0, lower[0])
    for p in range(1, planes):
        keep(lower_ref, 2 * p - 1, lower[p])
        keep(lower_ref, 2 * p, halves(product(halves(loff[p - 1]), lower[p])))
    merged = []
    for p in range(planes):
        keep(upper_ref, 2 * p, upper[p])
        if p < planes - 1:
            merged.append(product(halves(uoff[p]), upper[p]))
            keep(upper_ref, 2 * p + 1, halves(merged[p]))
    keep(back_ref, 0, upper[0])
    tail = None
    for p in range(1, planes):
        step = (-open_any[p]) * merged[p - 1]
        tail = halves(step if tail is None else product(halves(step), tail))
        keep(back_ref, p, halves(product(upper[p], tail)))
    forward_rows(copies, rhs, t_ref, gates[:count], lower_ref, back_ref, upper_ref, link, sep, m_ref, p_ref)


def forward_rest_kernel(
    rhs_hbm, sep_hbm, from_hbm, gates_ref, lower_ref, upper_ref, back_ref,
    m_ref, p_ref, t_ref,
    rhs, sep, link, sems,
):
    planes, count, _ = rhs.shape
    copies, fetch = fetcher(sems)
    for plane in range(planes):
        fetch(plane, rhs_hbm.at[plane, count:], rhs.at[plane])
    fetch("link", from_hbm.at[:, count:], link)
    fetch("sep", sep_hbm.at[0, count:], sep)
    forward_rows(copies, rhs, t_ref, gates_ref[count:], lower_ref, back_ref, upper_ref, link, sep, m_ref, p_ref)


def backward_kernel(
    ta_ref, tb_ref, gates_ref, lower_ref, upper_ref, back_ref, x_ref, apply_ref, sweep_ref, mask_ref
):
    planes, _, width = ta_ref.shape
    gates = gates_ref[...]
    like = (gates.shape[0], width)
    one = lambda ref, index: block(ref, index, 1)

    open_any = [jnp.max(gates[:, planes + p : planes + p + 1], axis=0, keepdims=True) for p in range(planes)]
    now = one(lower_ref, 0)
    last = one(lower_ref, 2 * planes - 3)
    for p in range(planes):
        if p > 0:
            now = halves((-open_any[p]) * product(now, one(lower_ref, 2 * p)))
        full = one(back_ref, p)
        keep(apply_ref, p, halves(product(now, full)))
        if p < planes - 1:
            keep(sweep_ref, 2 * p, halves(product(now, one(upper_ref, 2 * p))))
            keep(sweep_ref, 2 * p + 1, one(upper_ref, 2 * p + 1))
        else:
            keep(apply_ref, planes, halves(product(last, full)))
            keep(apply_ref, planes + 1, halves(product(last, one(upper_ref, 2 * p))))
            keep(apply_ref, planes + 2, halves(product(now, one(upper_ref, 2 * p))))

    def lowered(p):
        return halves(jnp.concatenate([ta_ref[p], tb_ref[p]], axis=0))

    solved = product(lowered(planes - 1), one(upper_ref, 2 * planes - 2))
    x_ref[planes - 1] = solved
    for p in range(planes - 2, -1, -1):
        mask = -column(gates, p, like)
        mask_ref[p] = mask
        solved = product(side(lowered(p), masked(halves(solved), mask)), block(upper_ref, 2 * p, 2))
        x_ref[p] = solved
    for p in range(1, planes):
        mask_ref[planes - 2 + p] = column(gates, planes + p, like)


def slab(vector, following, into_ref, mask_ref, apply_ref):
    planes = 8
    near = halves(into_ref[0] * vector)
    far = halves(into_ref[1] * following)
    gated = [near] + [masked(near, mask_ref[planes - 2 + p]) for p in range(1, planes)]
    far_end = product(side(far, gated[-1]), block(apply_ref, planes + 1, 2))
    near_end = product(masked(far, mask_ref[2 * planes - 3]), block(apply_ref, planes, 1))
    for p in range(0, planes, 2):
        near_end = near_end + product(side(gated[p], gated[p + 1]), block(apply_ref, p, 2))
    return near_end, far_end


def inner_stencil(vector, diagonal):
    zero_row = jnp.zeros_like(vector[:1])
    zero_column = jnp.zeros_like(vector[:, :1])
    up = jnp.concatenate([zero_row, vector[:-1]], axis=0)
    down = jnp.concatenate([vector[1:], zero_row], axis=0)
    left = jnp.concatenate([zero_column, vector[:, :-1]], axis=1)
    right = jnp.concatenate([vector[:, 1:], zero_column], axis=1)
    return (
        (diagonal - SHIFT) * vector
        - (up + down)
        - (1.0 + CONVECTION) * left
        - (1.0 - CONVECTION) * right
    )


def put_rims(fields, rims):
    row_first, row_last, column_first, column_last = rims
    for index, field in enumerate(fields):
        row_first[index : index + 1, :] = field[:1]
        row_last[index : index + 1, :] = field[-1:]
        turned = jnp.transpose(field)
        column_first[index : index + 1, :] = turned[:1]
        column_last[index : index + 1, :] = turned[-1:]


def rim_columns(flags, column_low, column_high):
    low = (1.0 + CONVECTION) * only(flags, LEFT, column_low[...])
    high = (1.0 - CONVECTION) * only(flags, RIGHT, column_high[...])
    return jnp.transpose(jnp.concatenate([low, high] * 2, axis=0))


def rim_terms(flags, index, rows, turned, row_low, row_high, width):
    start, stop, total = rows
    count = stop - start
    lane = lax.broadcasted_iota(jnp.int32, (count, width), 1)
    line = lax.broadcasted_iota(jnp.int32, (count, width), 0)
    low = turned[start:stop, index : index + 1]
    high = turned[start:stop, index + 2 : index + 3]
    value = jnp.where(lane == 0, low, jnp.where(lane == width - 1, high, 0.0))
    if start == 0:
        value = value + jnp.where(line == 0, only(flags, ABOVE, row_low[index : index + 1, :]), 0.0)
    if stop == total:
        value = value + jnp.where(line == count - 1, only(flags, BELOW, row_high[index : index + 1, :]), 0.0)
    return value


def first_kernel(
    pa, pb, ma, mb, ma_prev, mb_prev, pa_next, pb_next, into_ref, from_ref, diag_ref, mask_ref, apply_ref,
    k_ref, kn_ref, mm_ref, loc_ref, row_first, row_last, column_first, column_last,
):
    flags = neighbours()
    own = (pa[...] + only(flags, BEFORE, ma_prev[...]), pb[...] + only(flags, BEFORE, mb_prev[...]))
    other = (only(flags, AFTER, pa_next[...] + ma[...]), only(flags, AFTER, pb_next[...] + mb[...]))
    vector = jnp.concatenate(own, axis=0)
    following = jnp.concatenate(other, axis=0)
    k_ref[...] = vector
    kn_ref[...] = following
    put_rims((vector, following), (row_first, row_last, column_first, column_last))
    near, far = slab(vector, following, into_ref, mask_ref, apply_ref)
    mm_ref[...] = from_ref[1] * far
    loc_ref[...] = inner_stencil(vector, diag_ref[0]) - from_ref[0] * near


def second_kernel(
    loc_ref, mm_ref, mm_prev, loc_next, row_low, row_high, column_low, column_high,
    into_ref, from_ref, diag_ref, mask_ref, apply_ref, x0_ref,
    k_ref, kn_ref, mma_ref, mmb_ref, loca_ref, locb_ref, row_first, row_last, column_first, column_last,
):
    flags = neighbours()
    count, width = loc_ref.shape
    half = count // 2
    turned = rim_columns(flags, column_low, column_high)
    rows = (0, count, count)
    vector = loc_ref[...] - only(flags, BEFORE, mm_prev[...]) - rim_terms(flags, 0, rows, turned, row_low, row_high, width)
    following = loc_next[...] - mm_ref[...] - rim_terms(flags, 1, rows, turned, row_low, row_high, width)
    following = only(flags, AFTER, following)
    k_ref[...] = vector
    kn_ref[...] = following
    put_rims((vector, following), (row_first, row_last, column_first, column_last))
    near, far = slab(vector, following, into_ref, mask_ref, apply_ref)
    sent = from_ref[1] * far
    mma_ref[...] = sent[:half]
    mmb_ref[...] = sent[half:]
    local = inner_stencil(vector, diag_ref[0]) - from_ref[0] * near
    loca_ref[...] = local[:half]
    locb_ref[...] = local[half:]


def sums_kernel(
    k0, k0n, k1, k1n, mma, mmb_prev, loca, locb, loca_next, row_low, row_high, column_low, column_high, x0_ref, x1_ref,
    out_ref,
):
    flags = neighbours()
    count, width = k0.shape
    half = count // 2
    turned = rim_columns(flags, column_low, column_high)
    top, bottom = (0, half, count), (half, count, count)
    own_low = loca[...] - rim_terms(flags, 0, top, turned, row_low, row_high, width)
    own_high = locb[...] - only(flags, BEFORE, mmb_prev[...]) - rim_terms(flags, 0, bottom, turned, row_low, row_high, width)
    next_low = loca_next[...] - mma[...] - rim_terms(flags, 1, top, turned, row_low, row_high, width)
    groups = (
        (k0[half:], k1[half:] * SCALE_ONE, own_high * SCALE_TWO),
        (k0n[:half], k1n[:half] * SCALE_ONE, only(flags, AFTER, next_low) * SCALE_TWO),
        (k0[:half], k1[:half] * SCALE_ONE, own_low * SCALE_TWO),
    )
    totals = [0.0] * 6
    for ordinal, (zero, one, two) in enumerate(groups):
        pairs = ((zero, zero), (zero, one), (one, one), (zero, two), (one, two), (two, two))
        for index, (left, right) in enumerate(pairs):
            value = jnp.sum((left * right).reshape(half // 8, 8, width), axis=0)
            if ordinal == 2:
                value = jnp.where(flags[BEFORE], 0.0, value)
            totals[index] = totals[index] + value
    lane = lax.broadcasted_iota(jnp.int32, (1, width), 1)
    line = jnp.zeros((1, width), F32)
    for index in range(6):
        line = jnp.where(lane == index, jnp.sum(totals[index]), line)
    out_ref[...] = jnp.broadcast_to(line, out_ref.shape)


def weights(sums):
    g00, g01, g11, g02, g12, g22 = sums
    one, two = 1.0 / SCALE_ONE, 1.0 / SCALE_TWO
    ratio = SCALE_ONE / SCALE_TWO
    square = g00 + EPSILON
    beta = jnp.sqrt(square)
    g00, g01s, g11s = g00 / square, g01 / square, g11 / square
    g02s, g12s, g22s = g02 / square, g12 / square, g22 / square
    lag = EPSILON / square
    delta = g01s * one - SHIFT * lag
    h11 = delta + SHIFT
    small_delta = delta * SCALE_ONE
    qq = (g11s - 2.0 * small_delta * g01s + small_delta * small_delta * g00) * one * one
    qq = jnp.maximum(qq, 0.0)
    h21 = jnp.sqrt(qq + EPSILON)
    inverse = 1.0 / h21
    gap = delta / ratio
    ku = (g02s - gap * g01s) * (two * inverse)
    kq = h11 * lag * inverse
    h12 = ku + SHIFT * kq
    qu = (g12s - gap * g11s - small_delta * g02s + small_delta * gap * g01s) * one * inverse * (two * inverse)
    vv = qq * inverse * inverse
    h22 = qu + SHIFT * vv
    turn = h22 - SHIFT
    uu = (g22s - 2.0 * gap * g12s + gap * gap * g11s) * (two * inverse) * (two * inverse)
    rr = uu + turn * turn * vv + h12 * h12 * g00 - 2.0 * turn * qu - 2.0 * h12 * ku + 2.0 * turn * h12 * kq
    h32 = jnp.sqrt(jnp.maximum(rr, 0.0) + EPSILON)
    radius = jnp.sqrt(h11 * h11 + h21 * h21)
    cosine = h11 / radius
    sine = h21 / radius
    upper_entry = cosine * h12 + sine * h22
    lower_entry = cosine * h22 - sine * h12
    second = jnp.sqrt(lower_entry * lower_entry + h32 * h32)
    weight_two = -beta * sine * lower_entry / (second * second)
    weight_one = (beta * cosine - upper_entry * weight_two) / radius
    scaled_two = weight_two * inverse / beta
    return weight_one / beta - scaled_two * delta, scaled_two


def sweep_kernel(k, kn, into_ref, mask_ref, apply_ref, sweep_ref, x_ref):
    planes = x_ref.shape[0]
    near = halves(into_ref[0] * k[...])
    far = halves(into_ref[1] * kn[...])
    running = None
    for p in range(planes - 1, -1, -1):
        gated = near if p == 0 else masked(near, mask_ref[planes - 2 + p])
        if running is None:
            running = product(side(far, gated), block(apply_ref, planes + 1, 2))
        else:
            other = masked(halves(running), mask_ref[p])
            running = product(side(gated, other), block(sweep_ref, 2 * p, 2))
        x_ref[p] = running


def final_kernel(gathered, k0, k1, x_ref, x0_ref, x1_ref, out_hbm, sep_hbm, out, sep, sems):
    planes = x_ref.shape[0]
    line = jnp.sum(gathered[...], axis=0, keepdims=True)
    lane = lax.broadcasted_iota(jnp.int32, line.shape, 1)
    sums = [jnp.sum(jnp.where(lane == index, line, 0.0), axis=1, keepdims=True) for index in range(6)]
    one, two = weights(sums)
    copies = []
    for p in range(planes):
        out[p] = x_ref[p] + (one * x0_ref[p] + two * x1_ref[p])
        copies.append(pltpu.make_async_copy(out.at[p], out_hbm.at[p], sems.at[p]))
        copies[-1].start()
    sep[...] = one * k0[...] + two * k1[...]
    copies.append(pltpu.make_async_copy(sep, sep_hbm.at[0], sems.at[planes]))
    copies[-1].start()
    for copy in copies:
        copy.wait()


def inside(count):
    return [pl.BlockSpec(memory_space=pltpu.VMEM)] * count


def outside(count, space=pl.ANY):
    return [pl.BlockSpec(memory_space=space)] * count


def shape(*sizes, dtype=F32):
    return jax.ShapeDtypeStruct(sizes, dtype)


def call(kernel, name, in_specs, out_shape, out_specs, scratch=(), flops=0, moved=0):
    return pl.pallas_call(
        kernel,
        name=name,
        in_specs=in_specs,
        out_shape=out_shape,
        out_specs=out_specs,
        scratch_shapes=list(scratch),
        compiler_params=pltpu.CompilerParams(vmem_limit_bytes=LIMIT),
        cost_estimate=pl.CostEstimate(flops=flops, bytes_accessed=moved, transcendentals=0),
    )


def body(
    rhs_interior, rhs_sep, lower_inv, lower_off, upper_inv, upper_off, link_into, link_from, sep_diag, coupling
):
    planes, count, width = rhs_interior.shape
    half = count // 2
    slabs, blocks, lines = (lax.axis_size(axis) for axis in AXES)
    plane = shape(count, width)
    dense = 2 * 2 * count * width * width

    def along(value, axis, by):
        size = lax.axis_size(axis)
        return lax.ppermute(value, axis, [(i, (i + by) % size) for i in range(size)])

    def rims(row_first, row_last, column_first, column_last):
        return (
            along(row_last, "gy", 1),
            along(row_first, "gy", -1),
            along(column_last, "gz", 1),
            along(column_first, "gz", -1),
        )

    rim_shapes = [shape(2, width), shape(2, width), shape(2, count), shape(2, count)]

    def in_hbm(*arrays):
        return [pltpu.with_memory_space_constraint(array, pltpu.HBM) for array in arrays]

    part = shape(half, width)
    tall = shape(planes, half, width)

    def stack(number):
        return shape(2, number * width, width, dtype=BF16)

    staged = [
        pltpu.VMEM((half, width), F32),
        pltpu.VMEM((2, half, width), F32),
        pltpu.SemaphoreType.DMA((planes + 7,)),
    ]
    ma, pa, ta, gates, lower, upper, back = call(
        forward_kernel,
        "forward",
        outside(8, pltpu.HBM),
        [part, part, tall, shape(count, 2 * planes), stack(2 * planes - 1), stack(2 * planes - 1), stack(planes)],
        inside(7),
        [
            pltpu.VMEM((planes, half, width), F32),
            pltpu.VMEM((planes, width, width), F32),
            pltpu.VMEM((planes - 1, width, width), F32),
            pltpu.VMEM((planes, width, width), F32),
            pltpu.VMEM((planes - 1, width, width), F32),
            pltpu.VMEM((planes - 1, count // width, width), jnp.int32),
            *staged,
        ],
        flops=dense * 16,
        moved=8 << 20,
    )(
        *in_hbm(rhs_interior, lower_inv, lower_off, upper_inv, upper_off),
        *in_hbm(coupling.reshape(planes - 1, count // width, width), rhs_sep, link_from),
    )
    ma_prev = along(ma, "gx", 1)
    pa_next = along(pa, "gx", -1)
    mb, pb, tb = call(
        forward_rest_kernel,
        "forward_rest",
        outside(3, pltpu.HBM) + inside(4),
        [part, part, tall],
        inside(3),
        [pltpu.VMEM((planes, half, width), F32), *staged],
        flops=dense * 12,
        moved=4 << 20,
    )(*in_hbm(rhs_interior, rhs_sep, link_from), gates, lower, upper, back)
    mb_prev = along(mb, "gx", 1)
    pb_next = along(pb, "gx", -1)
    x, applied, swept, masks = call(
        backward_kernel,
        "backward",
        inside(6),
        [
            shape(planes, count, width),
            stack(planes + 3),
            stack(2 * planes - 2),
            shape(2 * planes - 2, count, width, dtype=BF16),
        ],
        inside(4),
        flops=dense * 20,
        moved=12 << 20,
    )(ta, tb, gates, lower, upper, back)
    k0, k0n, mm, loc, *edges = call(
        first_kernel,
        "first",
        inside(13),
        [plane] * 4 + rim_shapes,
        inside(8),
        flops=dense * 11,
        moved=4 << 20,
    )(pa, pb, ma, mb, ma_prev, mb_prev, pa_next, pb_next, link_into, link_from, sep_diag, masks, applied)
    mm_prev = along(mm, "gx", 1)
    loc_next = along(loc, "gx", -1)
    arrived = rims(*edges)

    def swept_field(name, k, kn):
        return call(
            sweep_kernel,
            name,
            inside(6),
            shape(planes, count, width),
            pl.BlockSpec(memory_space=pltpu.VMEM),
            flops=dense * 16,
            moved=8 << 20,
        )(k, kn, link_into, masks, applied, swept)

    x0 = swept_field("sweep_first", k0, k0n)
    k1, k1n, mma, mmb, loca, locb, *edges = call(
        second_kernel,
        "second",
        inside(13) + outside(1),
        [plane] * 2 + [part] * 4 + rim_shapes,
        inside(10),
        flops=dense * 11,
        moved=4 << 20,
    )(loc, mm, mm_prev, loc_next, *arrived, link_into, link_from, sep_diag, masks, applied, x0)
    mmb_prev = along(mmb, "gx", 1)
    loca_next = along(loca, "gx", -1)
    arrived = rims(*edges)
    x1 = swept_field("sweep_second", k1, k1n)
    line = call(
        sums_kernel,
        "sums",
        inside(13) + outside(2),
        shape(slabs * blocks * lines, width),
        pl.BlockSpec(memory_space=pltpu.VMEM),
        flops=dense,
        moved=4 << 20,
    )(k0, k0n, k1, k1n, mma, mmb_prev, loca, locb, loca_next, *arrived, x0, x1)
    gathered = lax.all_to_all(line, AXES, 0, 0, tiled=True)
    interior, separator = call(
        final_kernel,
        "final",
        inside(6),
        [shape(planes, count, width), shape(1, count, width)],
        outside(2),
        [
            pltpu.VMEM((planes, count, width), F32),
            pltpu.VMEM((count, width), F32),
            pltpu.SemaphoreType.DMA((planes + 1,)),
        ],
        flops=dense,
        moved=16 << 20,
    )(gathered, k0, k1, x, x0, x1)
    return interior, separator


def solution(mesh):
    field = P(*AXES)
    factor = P(*AXES, None, None)
    return jax.shard_map(
        body,
        mesh=mesh,
        in_specs=(field, field, factor, factor, factor, factor, field, field, field, P("gz", "gx", "gy")),
        out_specs=(field, field),
        check_vma=False,
    )
```
